128 devices in a mesh: gx: 8 (over z, core), gy: 8 (over y, x_lo), ta: 2 (over x_hi).
Axes of the slice: x: 4 (x_hi: 2, x_lo: 2; x = x_hi * 2 + x_lo), y: 4, z: 4, core: 2. Of those that a mesh axis runs over, the one named last changes fastest.
Arguments:
- elevations: float32 [1024, 512, 1024], P('gx', 'gy', 'ta'), may hold values from -6 to 6
- time_basis: float32 [1024, 32], P('ta'), may hold values from -0.1875 to 0.1875
- north_basis: float32 [512, 32], P('gy'), may hold values from -0.25 to 0.25
- east_basis: float32 [1024, 32], P('gx'), may hold values from -0.1875 to 0.1875
Outputs:
- core_unfolded: float32 [32, 1024], P(None, ('gx', 'gy', 'ta'))
- gram_matrix: float32 [1024, 1024], P(('gx', 'gy', 'ta'))
The draws below stay inside these ranges and needn't reach their ends.
All inputs are finite; a program needn't handle non-finite values.
Results may differ from the reference program's by a relative error of at most 0.00009.
Values sent between devices are 32-bit elements; how exact they have to be, the bound alone decides.
A program may use at most 64 MiB of HBM per device.

```python
import jax
import jax.numpy as jnp
from jax import lax

RANK = 32
NX = 1024
NY = 512
NT = 1024


def block_levels(own_key, shape, shards, low, high):
    factor_of, own = 1.0, jax.random.fold_in(own_key, 6)
    for dim, parts in shards:
        steps = jnp.exp(jax.random.uniform(jax.random.fold_in(own, dim), (parts,), jnp.float32, low / len(shards), high / len(shards)))
        factor_of = factor_of * jnp.repeat(steps, shape[dim] // parts).reshape([-1 if axis == dim else 1 for axis in range(len(shape))])
    return factor_of


def noise(stream_key, extent, deviation, reach, split=(), held_as=jnp.bfloat16):
    entries = jax.random.normal(stream_key, extent, jnp.float32) * deviation
    if len(split) > 0:
        entries = block_levels(stream_key, extent, split, -0.22, 0.18) * entries
    return jnp.clip(entries, min=-reach, max=reach).astype(held_as)


def setup_inputs(seed: int = 0) -> dict:
    key_of = jax.random.split(jax.random.key(seed), 5)
    elevations = noise(key_of[0], (NX, NY, NT), 1.0, 6.0, ((0, 8), (1, 8), (2, 2)), jnp.float32)
    time_basis = noise(key_of[1], (NT, RANK), NT ** -0.5, 0.1875, ((0, 2),), jnp.float32)
    north_basis = noise(key_of[2], (NY, RANK), NY ** -0.5, 0.25, ((0, 8),), jnp.float32)
    east_basis = noise(key_of[3], (NX, RANK), NX ** -0.5, 0.1875, ((0, 8),), jnp.float32)
    return {"elevations": elevations, "time_basis": time_basis, "north_basis": north_basis, "east_basis": east_basis}


def reference(elevations, time_basis, north_basis, east_basis):
    highest = lax.Precision.HIGHEST
    time_mode = jnp.einsum("xyt,tr->xyr", elevations, time_basis, precision=highest)
    partial_core = jnp.einsum("yp,xyq->xpq", north_basis, time_mode, precision=highest).reshape(NX, RANK * RANK)
    core_unfolded = jnp.dot(east_basis.T, partial_core, precision=highest)
    gram_matrix = jnp.dot(partial_core, partial_core.T, precision=highest) / (RANK * RANK)
    return core_unfolded, gram_matrix
```

```python
import functools

import jax
import jax.numpy as jnp
from jax import lax
from jax.experimental import pallas as pl
from jax.experimental.pallas import tpu as pltpu
from jax.sharding import PartitionSpec as P

F32 = jnp.float32
BF16 = jnp.bfloat16
MESH = pl.DeviceIdType.MESH
NN = (((1,), (0,)), ((), ()))
NT = (((1,), (1,)), ((), ()))
RING = (0, 1, 3, 2)
CHUNKS = 4
STEP = 8 // CHUNKS
ROUNDS = ((0, 1), (1, 2), (3, 1))
LEGS = ((0, 3), (3, 1))


def split(values):
    high = values.astype(BF16)
    return high, (values - high.astype(F32)).astype(BF16)


def dot(a, b, dims):
    return lax.dot_general(a, b, dims, preferred_element_type=F32)


def exchange(values, lane, unit, stages):
    for s in stages:
        low = (lane // (unit * s)) % 2 == 0
        out = list(values)
        for a in range(len(values)):
            if a & s:
                continue
            out[a] = jnp.where(low, values[a], pltpu.roll(values[a + s], unit * s, 1))
            out[a + s] = jnp.where(low, pltpu.roll(values[a], 128 - unit * s, 1), values[a + s])
        values = out
    return values


def kernel(
    elev, time_t, north_t, east_t, core_out, gram_out,
    slab, time_v, north_v, basis, send1, recv1, mid1, last1, send_last, recv_last,
    blocks, twin, easts, core_part, core_twin, send2, recv2, mid2, last2,
    slab_sem, small_sem, send1_sem, recv1_sem, mid1_sem, last1_sem, direct_send, direct_recv,
    block_send, block_recv, east_send, east_recv, core_send, core_recv,
    send2_sem, recv2_sem, mid2_sem, last2_sem,
):
    gx, gy, ta = lax.axis_index("gx"), lax.axis_index("gy"), lax.axis_index("ta")
    z, core = gx // 2, gx % 2
    y, x = gy // 2, ta * 2 + gy % 2

    def slab_copy(c):
        part = pl.ds(c * STEP, STEP)
        return pltpu.make_async_copy(elev.at[:, part], slab.at[:, part], slab_sem.at[c])

    small = [
        pltpu.make_async_copy(time_t, time_v, small_sem.at[0]),
        pltpu.make_async_copy(north_t, north_v, small_sem.at[1]),
        pltpu.make_async_copy(east_t, easts.at[0], small_sem.at[2]),
    ]
    for copy in small:
        copy.start()
    for c in range(2):
        slab_copy(c).start()

    plane, along_x, along_y, ring, across = [], [], [], [], []
    for slot in range(1, 16):
        y2, x2 = (y + slot // 4) % 4, (x + slot % 4) % 4
        plane.append((slot, (gx, y2 * 2 + x2 % 2, x2 // 2), y2, x2))
    for slot in range(1, 4):
        along_x.append((slot, plane[slot - 1][1], plane[slot - 1][3]))
        along_y.append((slot, plane[slot * 4 - 1][1], plane[slot * 4 - 1][2]))
        ring.append((slot, (((z + RING[slot]) % 4) * 2 + core, gy, ta)))
    for slot in range(4):
        x2 = (x + slot) % 4
        across.append((slot, (z * 2 + 1 - core, y * 2 + x2 % 2, x2 // 2), x2))
    other = across[0][1]
    barrier = pltpu.get_barrier_semaphore()
    for peer in plane + ring + across:
        pl.semaphore_signal(barrier, inc=1, device_id=peer[1], device_id_type=MESH)

    first_leg, second_leg = (along_x, along_y), (along_y, along_x)
    first_at, second_at = (x, y), (y, x)

    for copy in small:
        copy.wait()
    time_high, time_low = split(time_v[...])
    time_both = jnp.concatenate([time_high, time_low], 0)
    time_wide = time_high.astype(F32).T.astype(BF16)
    lane = lax.broadcasted_iota(jnp.int32, (32, 128), 1)

    def make_basis():
        row = lax.broadcasted_iota(jnp.int32, (32, 128), 0)
        spread = jnp.where(4 * ((lane % 32) // 4) + lane // 32 == row, 1.0, 0.0).astype(BF16)
        lane64 = lax.broadcasted_iota(jnp.int32, (64, 128), 1)
        for h, part in enumerate(split(north_v[...].T)):
            wide = dot(part, spread, NN)
            for x4 in range(4):
                own = jnp.where(lane64 % 4 == x4, wide, 0.0).astype(BF16)
                basis[pl.ds(x4 * 64, 64), pl.ds(h * 128, 128)] = own

    def over_time(g, b):
        high, low = split(slab[b, g])
        t = dot(time_both, high, NT)
        return t[:32] + t[32:] + dot(low, time_wide, NN).T

    def over_y(terms):
        high, low = zip(*[split(t) for t in terms])
        r = dot(jnp.concatenate(high, 0), basis[...], NN)
        r = r[:, :128] + r[:, 128:] + dot(jnp.concatenate(low, 0), basis[:, :128], NN)
        return exchange([r[32 * b : 32 * b + 32] for b in range(4)], lane, 32, (2, 1))

    def remote(src, dst, send_sem, recv_sem, device):
        return pltpu.make_async_remote_copy(
            src_ref=src, dst_ref=dst, send_sem=send_sem, recv_sem=recv_sem, device_id=device, device_id_type=MESH
        )

    def await_bytes(ref, sem):
        pltpu.make_async_copy(ref, ref, sem).wait()

    def finish(c, terms):
        for h in range(STEP):
            tiles = over_y(terms[h])
            for pg in range(4):
                for qg in range(4):
                    at = (qg % 2) * 2 + qg // 2
                    f, s = (at, pg) if h == 0 else (pg, at)
                    tile = tiles[pg][qg * 8 : qg * 8 + 8]
                    if c == CHUNKS - 1:
                        send_last[pg, at, h] = tile
                    else:
                        send1[c, h, f, s] = tile
        if c == 0:
            pl.semaphore_wait(barrier, 22)
        if c == CHUNKS - 1:
            for slot, device, y2, x2 in plane:
                remote(send_last.at[y2, x2], recv_last.at[slot], direct_send, direct_recv, device).start()
            return
        for h in range(2):
            for slot, device, at in first_leg[h]:
                remote(
                    send1.at[c, h, at], recv1.at[c, h, slot], send1_sem.at[c], recv1_sem.at[c], device
                ).start()

    def east_copy(slot, device):
        return remote(easts.at[0], easts.at[slot], east_send, east_recv, device)

    held = None
    for c in range(CHUNKS):
        slab_copy(c).wait()
        if c + 2 < CHUNKS:
            slab_copy(c + 2).start()
        terms = [[over_time(c * STEP + k, b) for b in range(4)] for k in range(STEP)]
        if c == 0:
            make_basis()
        else:
            finish(c - 1, held)
            if c == 1:
                for peer in ring:
                    east_copy(*peer).start()
        held = terms
    finish(CHUNKS - 1, held)

    for c in range(CHUNKS - 1):
        await_bytes(recv1.at[c, :, pl.ds(1, 3)], recv1_sem.at[c])
    for h in range(2):
        for c in range(CHUNKS - 1):
            total = send1[c, h, first_at[h]]
            for slot in range(1, 4):
                total = total + recv1[c, h, slot]
            for k in range(4):
                mid1[h, k, c] = total[k]
        for slot, device, at in second_leg[h]:
            remote(mid1.at[h, at], last1.at[h, slot], mid1_sem, last1_sem, device).start()
    tiles = []
    await_bytes(last1.at[:, pl.ds(1, 3)], last1_sem)
    for c in range(CHUNKS - 1):
        for h in range(2):
            total = mid1[h, second_at[h], c]
            for slot in range(1, 4):
                total = total + last1[h, slot, c]
            tiles.append(total)
    await_bytes(recv_last.at[pl.ds(1, 15)], direct_recv)
    for h in range(2):
        total = send_last[y, x, h]
        for slot in range(1, 16):
            total = total + recv_last[slot, h]
        tiles.append(total)
    lane8 = lax.broadcasted_iota(jnp.int32, (8, 128), 1)
    tiles = exchange(tiles, lane8, 4, (4, 2, 1))
    for i in range(8):
        blocks[0, pl.ds(i * 8, 8), :] = tiles[i]

    def block_copy(slot, device):
        return remote(blocks.at[0], blocks.at[slot], block_send.at[slot], block_recv.at[slot], device)

    twin_copy = remote(blocks.at[0], twin, block_send.at[0], block_recv.at[0], other)
    for peer in ring[::-1]:
        block_copy(*peer).start()
    twin_copy.start()

    def left_side(block):
        high, low = split(block.T)
        return jnp.concatenate([high, high, low], 1)

    lefts = [left_side(jnp.concatenate(tiles, 0))]
    for r, (start, count) in enumerate(ROUNDS):
        for slot in range(start, start + count):
            if slot > 0:
                block_copy(*ring[slot - 1]).wait_recv()
            high, low = split(blocks[slot])
            right = jnp.concatenate([high, low, high], 0)
            for h in range(2):
                if len(lefts) == h:
                    twin_copy.wait_recv()
                    lefts.append(left_side(twin[...]))
                part = dot(lefts[h], right, NN)
                for index in range(16):
                    pg, qg = index // 4, index % 4
                    at = (qg % 2) * 2 + qg // 2
                    f, s = (at, pg) if h == 0 else (pg, at)
                    send2[h, f, slot, s] = part[index * 8 : index * 8 + 8]
        slots = pl.ds(start, count)
        for h in range(2):
            for slot, device, at in first_leg[h]:
                remote(
                    send2.at[h, at, slots], recv2.at[h, slot, slots], send2_sem.at[r], recv2_sem.at[r], device
                ).start()

    await_bytes(easts.at[pl.ds(1, 3)], east_recv)
    rows = [
        jnp.concatenate(
            [blocks[slot, pl.ds(pl.multiple_of(i * 8, 8), 8), :] for i in (gx, z * 2 + 1 - core)], 0
        )
        for slot in range(4)
    ]
    core_sum = lax.dot_general(
        jnp.concatenate(rows, 1),
        jnp.concatenate([easts[slot] for slot in range(4)], 1),
        NT,
        precision=lax.Precision.HIGHEST,
        preferred_element_type=F32,
    )
    core_part[...] = jnp.zeros((8, 128), F32)
    core_part[:, :32] = core_sum[8:]
    core_copy = remote(core_part, core_twin, core_send, core_recv, other)
    core_copy.start()

    done = 0
    for leg, (start, count) in enumerate(LEGS):
        while done < len(ROUNDS) and ROUNDS[done][0] < start + count:
            await_bytes(recv2.at[:, pl.ds(1, 3), pl.ds(*ROUNDS[done])], recv2_sem.at[done])
            done += 1
        part = pl.ds(start, count)
        for h in range(2):
            for pair in range(start, start + count):
                total = send2[h, first_at[h], pair]
                for slot in range(1, 4):
                    total = total + recv2[h, slot, pair]
                for k in range(4):
                    mid2[h, k, pair] = total[k]
            for slot, device, at in (along_y, across)[h]:
                remote(
                    mid2.at[h, at, part], last2.at[h, slot, part], mid2_sem.at[leg, h], last2_sem.at[leg, h], device
                ).start()

    core_copy.wait_recv()
    core_out[...] = core_sum[:8] + core_twin[:, :32]

    inverse_count = 1.0 / 1024.0

    def final(slot, c, total):
        at = (((z + 4 - RING[slot]) % 4) * 2 + c) * 128
        gram_out[:, pl.ds(pl.multiple_of(at, 128), 128)] = total * inverse_count

    for leg, (start, count) in enumerate(LEGS):
        part = pl.ds(start, count)
        await_bytes(last2.at[0, pl.ds(1, 3), part], last2_sem.at[leg, 0])
        for slot in range(start, start + count):
            total = mid2[0, y, slot]
            for peer in range(1, 4):
                total = total + last2[0, peer, slot]
            final(slot, core, total)
        await_bytes(last2.at[1, :, part], last2_sem.at[leg, 1])
        for slot in range(start, start + count):
            total = last2[1, 0, slot]
            for peer in range(1, 4):
                total = total + last2[1, peer, slot]
            final(slot, 1 - core, total)

    for c in range(CHUNKS - 1):
        await_bytes(recv1.at[c, :, pl.ds(1, 3)], send1_sem.at[c])
    await_bytes(last1.at[:, pl.ds(1, 3)], mid1_sem)
    await_bytes(recv_last.at[pl.ds(1, 15)], direct_send)
    await_bytes(easts.at[pl.ds(1, 3)], east_send)
    for peer in ring:
        block_copy(*peer).wait_send()
    twin_copy.wait_send()
    core_copy.wait_send()
    for r, part in enumerate(ROUNDS):
        await_bytes(recv2.at[:, pl.ds(1, 3), pl.ds(*part)], send2_sem.at[r])
    for leg, (start, count) in enumerate(LEGS):
        await_bytes(last2.at[0, pl.ds(1, 3), pl.ds(start, count)], mid2_sem.at[leg, 0])
        await_bytes(last2.at[1, :, pl.ds(start, count)], mid2_sem.at[leg, 1])


def hand_over(core_in, gram_in, core_out, gram_out, sem):
    copies = [
        pltpu.make_async_copy(core_in, core_out, sem.at[0]),
        pltpu.make_async_copy(gram_in, gram_out, sem.at[1]),
    ]
    for copy in copies:
        copy.start()
    for copy in copies:
        copy.wait()


def shards(elevations, time_basis, north_basis, east_basis):
    dma = pltpu.SemaphoreType.DMA
    shapes = ((8, 32), (8, 1024))
    far = pl.BlockSpec(memory_space=pltpu.HBM)
    near = pl.BlockSpec(memory_space=pltpu.VMEM)
    legs = CHUNKS - 1
    core_t, gram = pl.pallas_call(
        kernel,
        out_shape=tuple(pltpu.VMEM(shape, F32) for shape in shapes),
        in_specs=[far] * 4,
        out_specs=(near, near),
        scratch_shapes=[
            pltpu.VMEM((4, 8, 256, 512), F32),
            pltpu.VMEM((32, 512), F32),
            pltpu.VMEM((32, 64), F32),
            pltpu.VMEM((256, 256), BF16),
            pltpu.VMEM((legs, 2, 4, 4, 8, 128), F32),
            pltpu.VMEM((legs, 2, 4, 4, 8, 128), F32),
            pltpu.VMEM((2, 4, legs, 8, 128), F32),
            pltpu.VMEM((2, 4, legs, 8, 128), F32),
            pltpu.VMEM((4, 4, STEP, 8, 128), F32),
            pltpu.VMEM((16, STEP, 8, 128), F32),
            pltpu.VMEM((4, 64, 128), F32),
            pltpu.VMEM((64, 128), F32),
            pltpu.VMEM((4, 32, 128), F32),
            pltpu.VMEM((8, 128), F32),
            pltpu.VMEM((8, 128), F32),
            pltpu.VMEM((2, 4, 4, 4, 8, 128), F32),
            pltpu.VMEM((2, 4, 4, 4, 8, 128), F32),
            pltpu.VMEM((2, 4, 4, 8, 128), F32),
            pltpu.VMEM((2, 4, 4, 8, 128), F32),
            dma((CHUNKS,)),
            dma((3,)),
            dma((legs,)),
            dma((legs,)),
            dma,
            dma,
            dma,
            dma,
            dma((4,)),
            dma((4,)),
            dma,
            dma,
            dma,
            dma,
            dma((3,)),
            dma((3,)),
            dma((2, 2)),
            dma((2, 2)),
        ],
        compiler_params=pltpu.CompilerParams(
            collective_id=0, has_side_effects=True, vmem_limit_bytes=59 << 20
        ),
    )(elevations.reshape(4, 8, 256, 512), time_basis.T, north_basis.T, east_basis.T)
    core_t, gram = pl.pallas_call(
        hand_over,
        out_shape=tuple(jax.ShapeDtypeStruct(shape, F32) for shape in shapes),
        in_specs=[near, near],
        out_specs=(far, far),
        scratch_shapes=[dma((2,))],
        compiler_params=pltpu.CompilerParams(vmem_limit_bytes=59 << 20),
    )(pltpu.with_memory_space_constraint(core_t, pltpu.VMEM), pltpu.with_memory_space_constraint(gram, pltpu.VMEM))
    return core_t.T, gram


def solution(mesh):
    in_specs = (P("gx", "gy", "ta"), P("ta", None), P("gy", None), P("gx", None))
    out_specs = (P(None, ("gx", "gy", "ta")), P(("gx", "gy", "ta"), None))
    return jax.shard_map(shards, mesh=mesh, in_specs=in_specs, out_specs=out_specs, check_vma=False)
```

```python
import functools

import jax
import jax.numpy as jnp
from jax import lax
from jax.experimental import pallas as pl
from jax.experimental.pallas import tpu as pltpu
from jax.sharding import PartitionSpec as P

F32 = jnp.float32
BF16 = jnp.bfloat16
MESH = pl.DeviceIdType.MESH
NN = (((1,), (0,)), ((), ()))
NT = (((1,), (1,)), ((), ()))
RING = (0, 1, 3, 2)
SIZES = (2, 2, 2, 2)
CHUNKS = tuple((sum(SIZES[:c]), SIZES[c]) for c in range(len(SIZES)))
EARLY = 2
ROUNDS = ((0, 3), (3, 1))


def split(values):
    high = values.astype(BF16)
    return high, (values - high.astype(F32)).astype(BF16)


def dot(a, b, dims):
    return lax.dot_general(a, b, dims, preferred_element_type=F32)


def exchange(values, lane, unit, stages):
    for s in stages:
        low = (lane // (unit * s)) % 2 == 0
        out = list(values)
        for a in range(len(values)):
            if a & s:
                continue
            out[a] = jnp.where(low, values[a], pltpu.roll(values[a + s], unit * s, 1))
            out[a + s] = jnp.where(low, pltpu.roll(values[a], 128 - unit * s, 1), values[a + s])
        values = out
    return values


def kernel(
    elev, time_t, north_t, east_t, core_out, gram_out,
    slab, time_v, north_v, basis, send1, recv1, gathered, twin, halves, columns, easts, core_part, core_twin, send2, recv2,
    slab_sem, small_sem, send1_sem, recv1_sem, gather_send, gather_recv, twin_send, twin_recv,
    east_send, east_recv, core_send, core_recv, send2_sem, recv2_sem,
):
    gx, gy, ta = lax.axis_index("gx"), lax.axis_index("gy"), lax.axis_index("ta")
    z, core = gx // 2, gx % 2
    y, x = gy // 2, ta * 2 + gy % 2
    twin_gx = z * 2 + 1 - core

    def slab_copy(c):
        part = pl.ds(*CHUNKS[c])
        return pltpu.make_async_copy(elev.at[:, part], slab.at[:, part], slab_sem.at[c])

    small = [
        pltpu.make_async_copy(time_t, time_v, small_sem.at[0]),
        pltpu.make_async_copy(north_t, north_v, small_sem.at[1]),
        pltpu.make_async_copy(east_t, easts.at[0], small_sem.at[2]),
    ]
    for copy in small:
        copy.start()
    for c in range(2):
        slab_copy(c).start()

    plane, along_x, sheet, across = [], [], [], []
    for slot in range(1, 16):
        y2, x2 = (y + slot // 4) % 4, (x + slot % 4) % 4
        plane.append((slot, (gx, y2 * 2 + x2 % 2, x2 // 2), y2, x2))
    for slot in range(1, 4):
        along_x.append((slot, plane[slot - 1][1], plane[slot - 1][3]))
    for zs in (3, 1, 2, 0):
        for ys in (2, 1, 3, 0):
            if zs or ys:
                y2 = (y + ys) % 4
                sheet.append((zs, (((z + RING[zs]) % 4) * 2 + core, y2 * 2 + gy % 2, ta)))
    for slot in range(4):
        x2 = (x + slot) % 4
        across.append((slot, (twin_gx, y * 2 + x2 % 2, x2 // 2), x2))
    other = across[0][1]
    ring = [(zs, (((z + RING[zs]) % 4) * 2 + core, gy, ta)) for zs in range(1, 4)]
    barrier = pltpu.get_barrier_semaphore()
    peers = [p[1] for p in plane + across] + [device for zs, device in sheet if zs]
    for device in peers:
        pl.semaphore_signal(barrier, inc=1, device_id=device, device_id_type=MESH)

    for copy in small:
        copy.wait()
    time_high, time_low = split(time_v[...])
    time_both = jnp.concatenate([time_high, time_low], 0)
    time_wide = time_high.astype(F32).T.astype(BF16)
    lane64 = lax.broadcasted_iota(jnp.int32, (64, 128), 1)

    def make_basis():
        row = lax.broadcasted_iota(jnp.int32, (32, 128), 0)
        lane = lax.broadcasted_iota(jnp.int32, (32, 128), 1)
        spread = jnp.where(lane // 4 == row, 1.0, 0.0).astype(BF16)
        for h, part in enumerate(split(north_v[...].T)):
            wide = dot(part, spread, NN)
            for x4 in range(4):
                own = jnp.where(lane64 % 4 == x4, wide, 0.0).astype(BF16)
                basis[pl.ds(x4 * 64, 64), pl.ds(h * 128, 128)] = own

    def over_time(g, b):
        high, low = split(slab[b, g])
        t = dot(time_both, high, NT)
        return t[:32] + t[32:] + dot(low, time_wide, NN).T

    def over_y(terms):
        high, low = zip(*[split(t) for t in terms])
        r = dot(jnp.concatenate(high, 0), basis[...], NN)
        return r[:, :128] + r[:, 128:] + dot(jnp.concatenate(low, 0), basis[:, :128], NN)

    def remote(src, dst, send_sem, recv_sem, device):
        return pltpu.make_async_remote_copy(
            src_ref=src, dst_ref=dst, send_sem=send_sem, recv_sem=recv_sem, device_id=device, device_id_type=MESH
        )

    def await_bytes(ref, sem):
        pltpu.make_async_copy(ref, ref, sem).wait()

    def place(qg):
        return (qg % 2) * 2 + qg // 2

    def finish(c, terms):
        start, count = CHUNKS[c]
        for k in range(count):
            sums = over_y(terms[k])
            for b in range(4):
                for qg in range(4):
                    at = b * 32 + qg * 8
                    send1[b, place(qg), start + k] = sums[at : at + 8]
        if c == 0:
            pl.semaphore_wait(barrier, 31)
        part = pl.ds(start, count)
        for slot, device, y2, x2 in plane:
            remote(
                send1.at[y2, x2, part], recv1.at[slot, part], send1_sem.at[c], recv1_sem.at[c], device
            ).start()
        if c == 0:
            for zs, device in ring:
                remote(easts.at[0], easts.at[zs], east_send, east_recv, device).start()

    held = None
    for c, (start, count) in enumerate(CHUNKS):
        slab_copy(c).wait()
        if c + 2 < len(CHUNKS):
            slab_copy(c + 2).start()
        if c > 1:
            finish(c - 1, held)
        held = [[over_time(start + k, b) for b in range(4)] for k in range(count)]
        if c == 0:
            make_basis()
            finish(0, held)
    finish(len(CHUNKS) - 1, held)

    lane8 = lax.broadcasted_iota(jnp.int32, (8, 128), 1)
    own = []
    for c, (start, count) in enumerate(CHUNKS):
        part = pl.ds(start, count)
        await_bytes(recv1.at[pl.ds(1, 15), part], recv1_sem.at[c])
        totals = []
        for g in range(start, start + count):
            total = send1[y, x, g]
            for slot in range(1, 16):
                total = total + recv1[slot, g]
            totals.append(total)
        totals = exchange(totals, lane8, 4, (1,))
        own += totals
        for k in range(count):
            gathered[0, y, start + k] = totals[k]
        for zs, device in sheet:
            remote(
                gathered.at[0, y, part], gathered.at[zs, y, part], gather_send, gather_recv.at[zs, c // EARLY], device
            ).start()
        remote(gathered.at[0, y, part], twin.at[part], twin_send, twin_recv, other).start()

    def left_side(tiles):
        turned = jnp.concatenate(exchange(tiles, lane8, 4, (4, 2)), 0).T
        high, low = split(jnp.concatenate([turned[32 * k : 32 * k + 32] for k in range(4)], 1))
        return jnp.concatenate([high, high, low], 1)

    def half(zs, h):
        by_y = [exchange([gathered[zs, y2, h * 4 + g] for g in range(4)], lane8, 4, (2,)) for y2 in range(4)]
        by_low = [exchange([by_y[y2][k] for y2 in range(4)], lane8, 32, (2, 1)) for k in range(4)]
        return [[by_low[k][high_p] for k in range(4)] for high_p in range(4)]

    def await_half(zs, h):
        ref = gathered.at[0, pl.ds(0, 3), pl.ds(0, 4)] if zs == 0 else gathered.at[zs, :, pl.ds(0, 4)]
        await_bytes(ref, gather_recv.at[zs, h])

    own_left = left_side(own)
    for zs in range(4):
        await_half(zs, 0)
    for zs in range(4):
        tiles = half(zs, 0)
        for high_p in range(4):
            for k in range(4):
                halves[zs, high_p, k] = tiles[high_p][k]
    await_bytes(twin, twin_recv)
    left = jnp.concatenate([own_left, left_side([twin[g] for g in range(8)])], 0)

    for r, (start, count) in enumerate(ROUNDS):
        for zs in range(start, start + count):
            await_half(zs, 1)
        for zs in range(start, start + count):
            second = half(zs, 1)
            tiles = [None] * 32
            for high_p in range(4):
                for k in range(4):
                    pair = exchange([halves[zs, high_p, k], second[high_p][k]], lane8, 16, (1,))
                    tiles[high_p * 8 + k], tiles[high_p * 8 + 4 + k] = pair
            for p in range(32):
                columns[zs, p] = tiles[p]
            high, low = split(jnp.concatenate(tiles, 0))
            product = dot(left, jnp.concatenate([high, low, high], 0), NN)
            for h in range(2):
                for qg in range(4):
                    at = h * 32 + qg * 8
                    send2[h, place(qg), zs] = product[at : at + 8]
        part = pl.ds(start, count)
        for h in range(2):
            for slot, device, at in (along_x, across)[h]:
                remote(
                    send2.at[h, at, part], recv2.at[h, slot, part], send2_sem.at[r, h], recv2_sem.at[r, h], device
                ).start()

    await_bytes(easts.at[pl.ds(1, 3)], east_recv)
    rows = [
        jnp.concatenate([columns[zs, 4 * gx + y], columns[zs, 4 * twin_gx + y]], 0) for zs in range(4)
    ]
    core_sum = lax.dot_general(
        jnp.concatenate(rows, 1),
        jnp.concatenate([easts[zs] for zs in range(4)], 1),
        NT,
        precision=lax.Precision.HIGHEST,
        preferred_element_type=F32,
    )
    core_part[...] = jnp.zeros((8, 128), F32)
    core_part[:, :32] = core_sum[8:]
    core_copy = remote(core_part, core_twin, core_send, core_recv, other)
    core_copy.start()
    core_copy.wait_recv()
    core_out[...] = core_sum[:8] + core_twin[:, :32]

    inverse_count = 1.0 / 1024.0

    def final(zs, c, total):
        at = (((z + 4 - RING[zs]) % 4) * 2 + c) * 128
        gram_out[:, pl.ds(pl.multiple_of(at, 128), 128)] = total * inverse_count

    for r, (start, count) in enumerate(ROUNDS):
        part = pl.ds(start, count)
        await_bytes(recv2.at[0, pl.ds(1, 3), part], recv2_sem.at[r, 0])
        for zs in range(start, start + count):
            total = send2[0, x, zs]
            for slot in range(1, 4):
                total = total + recv2[0, slot, zs]
            final(zs, core, total)
        await_bytes(recv2.at[1, :, part], recv2_sem.at[r, 1])
        for zs in range(start, start + count):
            total = recv2[1, 0, zs]
            for slot in range(1, 4):
                total = total + recv2[1, slot, zs]
            final(zs, 1 - core, total)

    for c, part in enumerate(CHUNKS):
        await_bytes(recv1.at[pl.ds(1, 15), pl.ds(*part)], send1_sem.at[c])
    await_bytes(recv1.at[pl.ds(1, 15)], gather_send)
    await_bytes(twin, twin_send)
    await_bytes(easts.at[pl.ds(1, 3)], east_send)
    core_copy.wait_send()
    for r, part in enumerate(ROUNDS):
        await_bytes(recv2.at[0, pl.ds(1, 3), pl.ds(*part)], send2_sem.at[r, 0])
        await_bytes(recv2.at[1, :, pl.ds(*part)], send2_sem.at[r, 1])


def hand_over(core_in, gram_in, core_out, gram_out, sem):
    copies = [
        pltpu.make_async_copy(core_in, core_out, sem.at[0]),
        pltpu.make_async_copy(gram_in, gram_out, sem.at[1]),
    ]
    for copy in copies:
        copy.start()
    for copy in copies:
        copy.wait()


def shards(elevations, time_basis, north_basis, east_basis):
    dma = pltpu.SemaphoreType.DMA
    shapes = ((8, 32), (8, 1024))
    far = pl.BlockSpec(memory_space=pltpu.HBM)
    near = pl.BlockSpec(memory_space=pltpu.VMEM)
    chunks = len(CHUNKS)
    core_t, gram = pl.pallas_call(
        kernel,
        out_shape=tuple(pltpu.VMEM(shape, F32) for shape in shapes),
        in_specs=[far] * 4,
        out_specs=(near, near),
        scratch_shapes=[
            pltpu.VMEM((4, 8, 256, 512), F32),
            pltpu.VMEM((32, 512), F32),
            pltpu.VMEM((32, 64), F32),
            pltpu.VMEM((256, 256), BF16),
            pltpu.VMEM((4, 4, 8, 8, 128), F32),
            pltpu.VMEM((16, 8, 8, 128), F32),
            pltpu.VMEM((4, 4, 8, 8, 128), F32),
            pltpu.VMEM((8, 8, 128), F32),
            pltpu.VMEM((4, 4, 4, 8, 128), F32),
            pltpu.VMEM((4, 32, 8, 128), F32),
            pltpu.VMEM((4, 32, 128), F32),
            pltpu.VMEM((8, 128), F32),
            pltpu.VMEM((8, 128), F32),
            pltpu.VMEM((2, 4, 4, 8, 128), F32),
            pltpu.VMEM((2, 4, 4, 8, 128), F32),
            dma((chunks,)),
            dma((3,)),
            dma((chunks,)),
            dma((chunks,)),
            dma,
            dma((4, 2)),
            dma,
            dma,
            dma,
            dma,
            dma,
            dma,
            dma((2, 2)),
            dma((2, 2)),
        ],
        compiler_params=pltpu.CompilerParams(
            collective_id=0, has_side_effects=True, vmem_limit_bytes=59 << 20
        ),
    )(elevations.reshape(4, 8, 256, 512), time_basis.T, north_basis.T, east_basis.T)
    core_t, gram = pl.pallas_call(
        hand_over,
        out_shape=tuple(jax.ShapeDtypeStruct(shape, F32) for shape in shapes),
        in_specs=[near, near],
        out_specs=(far, far),
        scratch_shapes=[dma((2,))],
        compiler_params=pltpu.CompilerParams(vmem_limit_bytes=59 << 20),
    )(pltpu.with_memory_space_constraint(core_t, pltpu.VMEM), pltpu.with_memory_space_constraint(gram, pltpu.VMEM))
    return core_t.T, gram


def solution(mesh):
    in_specs = (P("gx", "gy", "ta"), P("ta", None), P("gy", None), P("gx", None))
    out_specs = (P(None, ("gx", "gy", "ta")), P(("gx", "gy", "ta"), None))
    return jax.shard_map(shards, mesh=mesh, in_specs=in_specs, out_specs=out_specs, check_vma=False)
```

```python
import functools

import jax
import jax.numpy as jnp
from jax import lax
from jax.experimental import pallas as pl
from jax.experimental.pallas import tpu as pltpu
from jax.sharding import PartitionSpec as P

F32 = jnp.float32
BF16 = jnp.bfloat16
MESH = pl.DeviceIdType.MESH
NN = (((1,), (0,)), ((), ()))
NT = (((1,), (1,)), ((), ()))
SIZES = (2, 2, 2, 2)
CHUNKS = tuple((sum(SIZES[:c]), SIZES[c]) for c in range(len(SIZES)))
EARLY = 2
ROUNDS = ((0, 1), (1, 1))


def split(values):
    high = values.astype(BF16)
    return high, (values - high.astype(F32)).astype(BF16)


def dot(a, b, dims):
    return lax.dot_general(a, b, dims, preferred_element_type=F32)


def exchange(values, lane, unit, stages):
    for s in stages:
        low = (lane // (unit * s)) % 2 == 0
        out = list(values)
        for a in range(len(values)):
            if a & s:
                continue
            out[a] = jnp.where(low, values[a], pltpu.roll(values[a + s], unit * s, 1))
            out[a + s] = jnp.where(low, pltpu.roll(values[a], 128 - unit * s, 1), values[a + s])
        values = out
    return values


def kernel(
    elev, time_t, north_t, east_t, core_out, gram_out,
    slab, time_v, north_v, basis, send1, recv1, gathered, mate_tiles, halves, columns, easts, core_part, core_mates, send2, recv2,
    slab_sem, small_sem, send1_sem, recv1_sem, gather_send, gather_recv, mate_send, mate_recv,
    east_send, east_recv, core_send, core_recv, send2_sem, recv2_sem,
):
    gx, gy, ta = lax.axis_index("gx"), lax.axis_index("gy"), lax.axis_index("ta")
    z, core = gx // 2, gx % 2
    y, x = gy // 2, ta * 2 + gy % 2
    mates = [z2 * 2 + c2 for z2 in (z, z + 1 - 2 * (z % 2)) for c2 in (core, 1 - core)]

    def slab_copy(c):
        part = pl.ds(*CHUNKS[c])
        return pltpu.make_async_copy(elev.at[:, part], slab.at[:, part], slab_sem.at[c])

    small = [
        pltpu.make_async_copy(time_t, time_v, small_sem.at[0]),
        pltpu.make_async_copy(north_t, north_v, small_sem.at[1]),
        pltpu.make_async_copy(east_t, easts.at[0], small_sem.at[2]),
    ]
    for copy in small:
        copy.start()
    for c in range(2):
        slab_copy(c).start()

    plane, sheet = [], []
    for slot in range(1, 16):
        y2, x2 = (y + slot // 4) % 4, (x + slot % 4) % 4
        plane.append((slot, (gx, y2 * 2 + x2 % 2, x2 // 2), y2, x2))
    for zs in (1, 0):
        for ys in (2, 1, 3, 0):
            if zs or ys:
                y2 = (y + ys) % 4
                sheet.append((zs, ((gx + 4 * zs) % 8, y2 * 2 + gy % 2, ta)))
    rings = []
    for m in range(4):
        ring = []
        for slot in range(4):
            x2 = (x + slot) % 4
            ring.append((slot, (mates[m], y * 2 + x2 % 2, x2 // 2), x2))
        rings.append(ring if m else ring[1:])
    across = rings[1] + rings[2] + rings[3]
    barrier = pltpu.get_barrier_semaphore()
    peers = [p[1] for p in plane + across] + [device for zs, device in sheet if zs]
    for device in peers:
        pl.semaphore_signal(barrier, inc=1, device_id=device, device_id_type=MESH)

    for copy in small:
        copy.wait()
    time_high, time_low = split(time_v[...])
    time_both = jnp.concatenate([time_high, time_low], 0)
    time_wide = time_high.astype(F32).T.astype(BF16)
    lane64 = lax.broadcasted_iota(jnp.int32, (64, 128), 1)

    def make_basis():
        row = lax.broadcasted_iota(jnp.int32, (32, 128), 0)
        lane = lax.broadcasted_iota(jnp.int32, (32, 128), 1)
        spread = jnp.where(lane // 4 == row, 1.0, 0.0).astype(BF16)
        for h, part in enumerate(split(north_v[...].T)):
            wide = dot(part, spread, NN)
            for x4 in range(4):
                own = jnp.where(lane64 % 4 == x4, wide, 0.0).astype(BF16)
                basis[pl.ds(x4 * 64, 64), pl.ds(h * 128, 128)] = own

    def over_time(g, b):
        high, low = split(slab[b, g])
        t = dot(time_both, high, NT)
        return t[:32] + t[32:] + dot(low, time_wide, NN).T

    def over_y(terms):
        high, low = zip(*[split(t) for t in terms])
        r = dot(jnp.concatenate(high, 0), basis[...], NN)
        return r[:, :128] + r[:, 128:] + dot(jnp.concatenate(low, 0), basis[:, :128], NN)

    def remote(src, dst, send_sem, recv_sem, device):
        return pltpu.make_async_remote_copy(
            src_ref=src, dst_ref=dst, send_sem=send_sem, recv_sem=recv_sem, device_id=device, device_id_type=MESH
        )

    def await_bytes(ref, sem):
        pltpu.make_async_copy(ref, ref, sem).wait()

    def place(qg):
        return (qg % 2) * 2 + qg // 2

    def finish(c, terms):
        start, count = CHUNKS[c]
        for k in range(count):
            sums = over_y(terms[k])
            for b in range(4):
                for qg in range(4):
                    at = b * 32 + qg * 8
                    send1[b, place(qg), start + k] = sums[at : at + 8]
        if c == 0:
            pl.semaphore_wait(barrier, 31)
        part = pl.ds(start, count)
        for slot, device, y2, x2 in plane:
            remote(
                send1.at[y2, x2, part], recv1.at[slot, part], send1_sem.at[c], recv1_sem.at[c], device
            ).start()
        if c == 0:
            for zs, device in sheet[3:4]:
                remote(easts.at[0], easts.at[1], east_send, east_recv, device).start()

    held = None
    for c, (start, count) in enumerate(CHUNKS):
        slab_copy(c).wait()
        if c + 2 < len(CHUNKS):
            slab_copy(c + 2).start()
        if c > 1:
            finish(c - 1, held)
        held = [[over_time(start + k, b) for b in range(4)] for k in range(count)]
        if c == 0:
            make_basis()
            finish(0, held)
    finish(len(CHUNKS) - 1, held)

    lane8 = lax.broadcasted_iota(jnp.int32, (8, 128), 1)
    own = []
    for c, (start, count) in enumerate(CHUNKS):
        part = pl.ds(start, count)
        await_bytes(recv1.at[pl.ds(1, 15), part], recv1_sem.at[c])
        totals = []
        for g in range(start, start + count):
            total = send1[y, x, g]
            for slot in range(1, 16):
                total = total + recv1[slot, g]
            totals.append(total)
        totals = exchange(totals, lane8, 4, (1,))
        own += totals
        for k in range(count):
            gathered[0, y, start + k] = totals[k]
        for zs, device in sheet:
            remote(
                gathered.at[0, y, part], gathered.at[zs, y, part], gather_send, gather_recv.at[zs, c // EARLY], device
            ).start()
        for m in range(1, 4):
            remote(gathered.at[0, y, part], mate_tiles.at[m - 1, part], mate_send, mate_recv, rings[m][0][1]).start()

    def left_side(tiles):
        turned = jnp.concatenate(exchange(tiles, lane8, 4, (4, 2)), 0).T
        high, low = split(jnp.concatenate([turned[32 * k : 32 * k + 32] for k in range(4)], 1))
        return jnp.concatenate([high, high, low], 1)

    def half(zs, h):
        by_y = [exchange([gathered[zs, y2, h * 4 + g] for g in range(4)], lane8, 4, (2,)) for y2 in range(4)]
        by_low = [exchange([by_y[y2][k] for y2 in range(4)], lane8, 32, (2, 1)) for k in range(4)]
        return [[by_low[k][high_p] for k in range(4)] for high_p in range(4)]

    def await_half(zs, h):
        ref = gathered.at[0, pl.ds(0, 3), pl.ds(0, 4)] if zs == 0 else gathered.at[zs, :, pl.ds(0, 4)]
        await_bytes(ref, gather_recv.at[zs, h])

    lefts = [left_side(own)]
    for zs in range(2):
        await_half(zs, 0)
    for zs in range(2):
        tiles = half(zs, 0)
        for high_p in range(4):
            for k in range(4):
                halves[zs, high_p, k] = tiles[high_p][k]
    await_bytes(mate_tiles, mate_recv)
    for m in range(3):
        lefts.append(left_side([mate_tiles[m, g] for g in range(8)]))
    left = jnp.concatenate(lefts, 0)

    for r, (start, count) in enumerate(ROUNDS):
        for zs in range(start, start + count):
            await_half(zs, 1)
        for zs in range(start, start + count):
            second = half(zs, 1)
            tiles = [None] * 32
            for high_p in range(4):
                for k in range(4):
                    pair = exchange([halves[zs, high_p, k], second[high_p][k]], lane8, 16, (1,))
                    tiles[high_p * 8 + k], tiles[high_p * 8 + 4 + k] = pair
            for p in range(32):
                columns[zs, p] = tiles[p]
            high, low = split(jnp.concatenate(tiles, 0))
            product = dot(left, jnp.concatenate([high, low, high], 0), NN)
            for m in range(4):
                for qg in range(4):
                    at = m * 32 + qg * 8
                    send2[m, place(qg), zs] = product[at : at + 8]
        part = pl.ds(start, count)
        for m in (3, 2, 1, 0):
            for slot, device, at in rings[m]:
                remote(
                    send2.at[m, at, part], recv2.at[m, slot, part], send2_sem.at[r, m], recv2_sem.at[r, m], device
                ).start()

    await_bytes(easts.at[1], east_recv)
    rows = [jnp.concatenate([columns[zs, 4 * mates[m] + y] for m in range(4)], 0) for zs in range(2)]
    core_sum = lax.dot_general(
        jnp.concatenate(rows, 1),
        jnp.concatenate([easts[zs] for zs in range(2)], 1),
        NT,
        precision=lax.Precision.HIGHEST,
        preferred_element_type=F32,
    )
    core_part[...] = jnp.zeros((3, 8, 128), F32)
    core_copies = []
    for m in range(1, 4):
        core_part[m - 1, :, :32] = core_sum[8 * m : 8 * m + 8]
        core_copies.append(
            remote(core_part.at[m - 1], core_mates.at[m - 1], core_send.at[m - 1], core_recv.at[m - 1], rings[m][0][1])
        )
    for copy in core_copies:
        copy.start()
    total = core_sum[:8]
    for m in range(3):
        core_copies[m].wait_recv()
        total = total + core_mates[m, :, :32]
    core_out[...] = total

    inverse_count = 1.0 / 1024.0

    for r, (start, count) in enumerate(ROUNDS):
        part = pl.ds(start, count)
        for m in range(4):
            peers = range(4) if m else range(1, 4)
            await_bytes(recv2.at[m, pl.ds(peers[0], len(peers)), part], recv2_sem.at[r, m])
            for zs in range(start, start + count):
                total = recv2[m, 0, zs] if m else send2[0, x, zs]
                for slot in range(1, 4):
                    total = total + recv2[m, slot, zs]
                at = ((mates[m] + 4 * zs) % 8) * 128
                gram_out[:, pl.ds(pl.multiple_of(at, 128), 128)] = total * inverse_count

    for c, part in enumerate(CHUNKS):
        await_bytes(recv1.at[pl.ds(1, 15), pl.ds(*part)], send1_sem.at[c])
    await_bytes(recv1.at[pl.ds(1, 7)], gather_send)
    await_bytes(mate_tiles, mate_send)
    await_bytes(easts.at[1], east_send)
    for copy in core_copies:
        copy.wait_send()
    for r, part in enumerate(ROUNDS):
        for m in range(4):
            peers = range(4) if m else range(1, 4)
            await_bytes(recv2.at[m, pl.ds(peers[0], len(peers)), pl.ds(*part)], send2_sem.at[r, m])


def hand_over(core_in, gram_in, core_out, gram_out, sem):
    copies = [
        pltpu.make_async_copy(core_in, core_out, sem.at[0]),
        pltpu.make_async_copy(gram_in, gram_out, sem.at[1]),
    ]
    for copy in copies:
        copy.start()
    for copy in copies:
        copy.wait()


def shards(elevations, time_basis, north_basis, east_basis):
    dma = pltpu.SemaphoreType.DMA
    shapes = ((8, 32), (8, 1024))
    far = pl.BlockSpec(memory_space=pltpu.HBM)
    near = pl.BlockSpec(memory_space=pltpu.VMEM)
    chunks = len(CHUNKS)
    core_t, gram = pl.pallas_call(
        kernel,
        out_shape=tuple(pltpu.VMEM(shape, F32) for shape in shapes),
        in_specs=[far] * 4,
        out_specs=(near, near),
        scratch_shapes=[
            pltpu.VMEM((4, 8, 256, 512), F32),
            pltpu.VMEM((32, 512), F32),
            pltpu.VMEM((32, 64), F32),
            pltpu.VMEM((256, 256), BF16),
            pltpu.VMEM((4, 4, 8, 8, 128), F32),
            pltpu.VMEM((16, 8, 8, 128), F32),
            pltpu.VMEM((2, 4, 8, 8, 128), F32),
            pltpu.VMEM((3, 8, 8, 128), F32),
            pltpu.VMEM((2, 4, 4, 8, 128), F32),
            pltpu.VMEM((2, 32, 8, 128), F32),
            pltpu.VMEM((2, 32, 128), F32),
            pltpu.VMEM((3, 8, 128), F32),
            pltpu.VMEM((3, 8, 128), F32),
            pltpu.VMEM((4, 4, 2, 8, 128), F32),
            pltpu.VMEM((4, 4, 2, 8, 128), F32),
            dma((chunks,)),
            dma((3,)),
            dma((chunks,)),
            dma((chunks,)),
            dma,
            dma((2, 2)),
            dma,
            dma,
            dma,
            dma,
            dma((3,)),
            dma((3,)),
            dma((2, 4)),
            dma((2, 4)),
        ],
        compiler_params=pltpu.CompilerParams(
            collective_id=0, has_side_effects=True, vmem_limit_bytes=59 << 20
        ),
    )(elevations.reshape(4, 8, 256, 512), time_basis.T, north_basis.T, east_basis.T)
    core_t, gram = pl.pallas_call(
        hand_over,
        out_shape=tuple(jax.ShapeDtypeStruct(shape, F32) for shape in shapes),
        in_specs=[near, near],
        out_specs=(far, far),
        scratch_shapes=[dma((2,))],
        compiler_params=pltpu.CompilerParams(vmem_limit_bytes=59 << 20),
    )(pltpu.with_memory_space_constraint(core_t, pltpu.VMEM), pltpu.with_memory_space_constraint(gram, pltpu.VMEM))
    return core_t.T, gram


def solution(mesh):
    in_specs = (P("gx", "gy", "ta"), P("ta", None), P("gy", None), P("gx", None))
    out_specs = (P(None, ("gx", "gy", "ta")), P(("gx", "gy", "ta"), None))
    return jax.shard_map(shards, mesh=mesh, in_specs=in_specs, out_specs=out_specs, check_vma=False)
```

```python
import functools

import jax
import jax.numpy as jnp
from jax import lax
from jax.experimental import pallas as pl
from jax.experimental.pallas import tpu as pltpu
from jax.sharding import PartitionSpec as P

F32 = jnp.float32
BF16 = jnp.bfloat16
MESH = pl.DeviceIdType.MESH
NN = (((1,), (0,)), ((), ()))
NT = (((1,), (1,)), ((), ()))
SIZES = (2, 2, 2, 2)
CHUNKS = tuple((sum(SIZES[:c]), SIZES[c]) for c in range(len(SIZES)))
EARLY = 2
ROUNDS = ((0, 1), (1, 1))


def split(values):
    high = values.astype(BF16)
    return high, (values - high.astype(F32)).astype(BF16)


def dot(a, b, dims):
    return lax.dot_general(a, b, dims, preferred_element_type=F32)


def exchange(values, lane, unit, stages):
    for s in stages:
        low = (lane // (unit * s)) % 2 == 0
        out = list(values)
        for a in range(len(values)):
            if a & s:
                continue
            out[a] = jnp.where(low, values[a], pltpu.roll(values[a + s], unit * s, 1))
            out[a + s] = jnp.where(low, pltpu.roll(values[a], 128 - unit * s, 1), values[a + s])
        values = out
    return values


def kernel(
    elev, time_t, north_t, east_t, core_out, gram_out,
    slab, time_v, north_v, basis, send1, recv1, gathered, mate_tiles, halves, columns, easts, core_part, core_mates, send2, recv2,
    slab_sem, small_sem, send1_sem, recv1_sem, gather_send, gather_recv, mate_send, mate_recv,
    east_send, east_recv, core_send, core_recv, send2_sem, recv2_sem,
):
    gx, gy, ta = lax.axis_index("gx"), lax.axis_index("gy"), lax.axis_index("ta")
    z, core = gx // 2, gx % 2
    y, x = gy // 2, ta * 2 + gy % 2
    near, beyond = z + 1 - 2 * (z % 2), (z + 3 + 2 * (z % 2)) % 4
    mates = [z2 * 2 + c2 for z2 in (z, near) for c2 in (core, 1 - core)]
    gathered_by = [(z2 * 2 + c2, z3 * 2 + c2) for z2, z3 in ((z, beyond), (near, (z + 2) % 4)) for c2 in (core, 1 - core)]

    def slab_copy(c):
        part = pl.ds(*CHUNKS[c])
        return pltpu.make_async_copy(elev.at[:, part], slab.at[:, part], slab_sem.at[c])

    small = [
        pltpu.make_async_copy(time_t, time_v, small_sem.at[0]),
        pltpu.make_async_copy(north_t, north_v, small_sem.at[1]),
        pltpu.make_async_copy(east_t, easts.at[0], small_sem.at[2]),
    ]
    for copy in small:
        copy.start()
    for c in range(2):
        slab_copy(c).start()

    plane, sheet = [], []
    for slot in range(1, 16):
        y2, x2 = (y + slot // 4) % 4, (x + slot % 4) % 4
        plane.append((slot, (gx, y2 * 2 + x2 % 2, x2 // 2), y2, x2))
    for zs in (1, 0):
        for ys in (2, 1, 3, 0):
            if zs or ys:
                y2 = (y + ys) % 4
                sheet.append((zs, (gathered_by[0][zs], y2 * 2 + gy % 2, ta)))
    rings = []
    for m in range(4):
        ring = []
        for slot in range(4):
            x2 = (x + slot) % 4
            ring.append((slot, (mates[m], y * 2 + x2 % 2, x2 // 2), x2))
        rings.append(ring if m else ring[1:])
    across = rings[1] + rings[2] + rings[3]
    barrier = pltpu.get_barrier_semaphore()
    peers = [p[1] for p in plane + across] + [device for zs, device in sheet if zs]
    for device in peers:
        pl.semaphore_signal(barrier, inc=1, device_id=device, device_id_type=MESH)

    for copy in small:
        copy.wait()
    time_high, time_low = split(time_v[...])
    time_both = jnp.concatenate([time_high, time_low], 0)
    time_wide = time_high.astype(F32).T.astype(BF16)
    lane64 = lax.broadcasted_iota(jnp.int32, (64, 128), 1)

    def make_basis():
        row = lax.broadcasted_iota(jnp.int32, (32, 128), 0)
        lane = lax.broadcasted_iota(jnp.int32, (32, 128), 1)
        spread = jnp.where(lane // 4 == row, 1.0, 0.0).astype(BF16)
        for h, part in enumerate(split(north_v[...].T)):
            wide = dot(part, spread, NN)
            for x4 in range(4):
                own = jnp.where(lane64 % 4 == x4, wide, 0.0).astype(BF16)
                basis[pl.ds(x4 * 64, 64), pl.ds(h * 128, 128)] = own

    def over_time(g, b):
        high, low = split(slab[b, g])
        t = dot(time_both, high, NT)
        return t[:32] + t[32:] + dot(low, time_wide, NN).T

    def over_y(terms):
        high, low = zip(*[split(t) for t in terms])
        r = dot(jnp.concatenate(high, 0), basis[...], NN)
        return r[:, :128] + r[:, 128:] + dot(jnp.concatenate(low, 0), basis[:, :128], NN)

    def remote(src, dst, send_sem, recv_sem, device):
        return pltpu.make_async_remote_copy(
            src_ref=src, dst_ref=dst, send_sem=send_sem, recv_sem=recv_sem, device_id=device, device_id_type=MESH
        )

    def await_bytes(ref, sem):
        pltpu.make_async_copy(ref, ref, sem).wait()

    def place(qg):
        return (qg % 2) * 2 + qg // 2

    def finish(c, terms):
        start, count = CHUNKS[c]
        for k in range(count):
            sums = over_y(terms[k])
            for b in range(4):
                for qg in range(4):
                    at = b * 32 + qg * 8
                    send1[b, place(qg), start + k] = sums[at : at + 8]
        if c == 0:
            pl.semaphore_wait(barrier, 31)
        part = pl.ds(start, count)
        for slot, device, y2, x2 in plane:
            remote(
                send1.at[y2, x2, part], recv1.at[slot, part], send1_sem.at[c], recv1_sem.at[c], device
            ).start()
        if c == 0:
            for zs, device in sheet[3:4]:
                remote(easts.at[0], easts.at[1], east_send, east_recv, device).start()

    held = None
    for c, (start, count) in enumerate(CHUNKS):
        slab_copy(c).wait()
        if c + 2 < len(CHUNKS):
            slab_copy(c + 2).start()
        if c > 1:
            finish(c - 1, held)
        held = [[over_time(start + k, b) for b in range(4)] for k in range(count)]
        if c == 0:
            make_basis()
            finish(0, held)
    finish(len(CHUNKS) - 1, held)

    lane8 = lax.broadcasted_iota(jnp.int32, (8, 128), 1)
    own = []
    for c, (start, count) in enumerate(CHUNKS):
        part = pl.ds(start, count)
        await_bytes(recv1.at[pl.ds(1, 15), part], recv1_sem.at[c])
        totals = []
        for g in range(start, start + count):
            total = send1[y, x, g]
            for slot in range(1, 16):
                total = total + recv1[slot, g]
            totals.append(total)
        totals = exchange(totals, lane8, 4, (1,))
        own += totals
        for k in range(count):
            gathered[0, y, start + k] = totals[k]
        for zs, device in sheet:
            remote(
                gathered.at[0, y, part], gathered.at[zs, y, part], gather_send, gather_recv.at[zs, c // EARLY], device
            ).start()
        for m in range(1, 4):
            remote(gathered.at[0, y, part], mate_tiles.at[m - 1, part], mate_send, mate_recv, rings[m][0][1]).start()

    def left_side(tiles):
        turned = jnp.concatenate(exchange(tiles, lane8, 4, (4, 2)), 0).T
        high, low = split(jnp.concatenate([turned[32 * k : 32 * k + 32] for k in range(4)], 1))
        return jnp.concatenate([high, high, low], 1)

    def half(zs, h):
        by_y = [exchange([gathered[zs, y2, h * 4 + g] for g in range(4)], lane8, 4, (2,)) for y2 in range(4)]
        by_low = [exchange([by_y[y2][k] for y2 in range(4)], lane8, 32, (2, 1)) for k in range(4)]
        return [[by_low[k][high_p] for k in range(4)] for high_p in range(4)]

    def await_half(zs, h):
        ref = gathered.at[0, pl.ds(0, 3), pl.ds(0, 4)] if zs == 0 else gathered.at[zs, :, pl.ds(0, 4)]
        await_bytes(ref, gather_recv.at[zs, h])

    lefts = [left_side(own)]
    for zs in range(2):
        await_half(zs, 0)
    for zs in range(2):
        tiles = half(zs, 0)
        for high_p in range(4):
            for k in range(4):
                halves[zs, high_p, k] = tiles[high_p][k]
    await_bytes(mate_tiles, mate_recv)
    for m in range(3):
        lefts.append(left_side([mate_tiles[m, g] for g in range(8)]))
    left = jnp.concatenate(lefts, 0)

    for r, (start, count) in enumerate(ROUNDS):
        for zs in range(start, start + count):
            await_half(zs, 1)
        for zs in range(start, start + count):
            second = half(zs, 1)
            tiles = [None] * 32
            for high_p in range(4):
                for k in range(4):
                    pair = exchange([halves[zs, high_p, k], second[high_p][k]], lane8, 16, (1,))
                    tiles[high_p * 8 + k], tiles[high_p * 8 + 4 + k] = pair
            for p in range(32):
                columns[zs, p] = tiles[p]
            high, low = split(jnp.concatenate(tiles, 0))
            product = dot(left, jnp.concatenate([high, low, high], 0), NN)
            for m in range(4):
                for qg in range(4):
                    at = m * 32 + qg * 8
                    send2[m, place(qg), zs] = product[at : at + 8]
        part = pl.ds(start, count)
        for m in (3, 2, 1, 0):
            for slot, device, at in rings[m]:
                remote(
                    send2.at[m, at, part], recv2.at[m, slot, part], send2_sem.at[r, m], recv2_sem.at[r, m], device
                ).start()

    await_bytes(easts.at[1], east_recv)
    rows = [jnp.concatenate([columns[zs, 4 * mates[m] + y] for m in range(4)], 0) for zs in range(2)]
    core_sum = lax.dot_general(
        jnp.concatenate(rows, 1),
        jnp.concatenate([easts[zs] for zs in range(2)], 1),
        NT,
        precision=lax.Precision.HIGHEST,
        preferred_element_type=F32,
    )
    core_part[...] = jnp.zeros((3, 8, 128), F32)
    core_copies = []
    for m in range(1, 4):
        core_part[m - 1, :, :32] = core_sum[8 * m : 8 * m + 8]
        core_copies.append(
            remote(core_part.at[m - 1], core_mates.at[m - 1], core_send.at[m - 1], core_recv.at[m - 1], rings[m][0][1])
        )
    for copy in core_copies:
        copy.start()
    total = core_sum[:8]
    for m in range(3):
        core_copies[m].wait_recv()
        total = total + core_mates[m, :, :32]
    core_out[...] = total

    inverse_count = 1.0 / 1024.0

    for r, (start, count) in enumerate(ROUNDS):
        part = pl.ds(start, count)
        for m in range(4):
            peers = range(4) if m else range(1, 4)
            await_bytes(recv2.at[m, pl.ds(peers[0], len(peers)), part], recv2_sem.at[r, m])
            for zs in range(start, start + count):
                total = recv2[m, 0, zs] if m else send2[0, x, zs]
                for slot in range(1, 4):
                    total = total + recv2[m, slot, zs]
                at = gathered_by[m][zs] * 128
                gram_out[:, pl.ds(pl.multiple_of(at, 128), 128)] = total * inverse_count

    for c, part in enumerate(CHUNKS):
        await_bytes(recv1.at[pl.ds(1, 15), pl.ds(*part)], send1_sem.at[c])
    await_bytes(recv1.at[pl.ds(1, 7)], gather_send)
    await_bytes(mate_tiles, mate_send)
    await_bytes(easts.at[1], east_send)
    for copy in core_copies:
        copy.wait_send()
    for r, part in enumerate(ROUNDS):
        for m in range(4):
            peers = range(4) if m else range(1, 4)
            await_bytes(recv2.at[m, pl.ds(peers[0], len(peers)), pl.ds(*part)], send2_sem.at[r, m])


def hand_over(core_in, gram_in, core_out, gram_out, sem):
    copies = [
        pltpu.make_async_copy(core_in, core_out, sem.at[0]),
        pltpu.make_async_copy(gram_in, gram_out, sem.at[1]),
    ]
    for copy in copies:
        copy.start()
    for copy in copies:
        copy.wait()


def shards(elevations, time_basis, north_basis, east_basis):
    dma = pltpu.SemaphoreType.DMA
    shapes = ((8, 32), (8, 1024))
    far = pl.BlockSpec(memory_space=pltpu.HBM)
    near = pl.BlockSpec(memory_space=pltpu.VMEM)
    chunks = len(CHUNKS)
    core_t, gram = pl.pallas_call(
        kernel,
        out_shape=tuple(pltpu.VMEM(shape, F32) for shape in shapes),
        in_specs=[far] * 4,
        out_specs=(near, near),
        scratch_shapes=[
            pltpu.VMEM((4, 8, 256, 512), F32),
            pltpu.VMEM((32, 512), F32),
            pltpu.VMEM((32, 64), F32),
            pltpu.VMEM((256, 256), BF16),
            pltpu.VMEM((4, 4, 8, 8, 128), F32),
            pltpu.VMEM((16, 8, 8, 128), F32),
            pltpu.VMEM((2, 4, 8, 8, 128), F32),
            pltpu.VMEM((3, 8, 8, 128), F32),
            pltpu.VMEM((2, 4, 4, 8, 128), F32),
            pltpu.VMEM((2, 32, 8, 128), F32),
            pltpu.VMEM((2, 32, 128), F32),
            pltpu.VMEM((3, 8, 128), F32),
            pltpu.VMEM((3, 8, 128), F32),
            pltpu.VMEM((4, 4, 2, 8, 128), F32),
            pltpu.VMEM((4, 4, 2, 8, 128), F32),
            dma((chunks,)),
            dma((3,)),
            dma((chunks,)),
            dma((chunks,)),
            dma,
            dma((2, 2)),
            dma,
            dma,
            dma,
            dma,
            dma((3,)),
            dma((3,)),
            dma((2, 4)),
            dma((2, 4)),
        ],
        compiler_params=pltpu.CompilerParams(
            collective_id=0, has_side_effects=True, vmem_limit_bytes=59 << 20
        ),
    )(elevations.reshape(4, 8, 256, 512), time_basis.T, north_basis.T, east_basis.T)
    core_t, gram = pl.pallas_call(
        hand_over,
        out_shape=tuple(jax.ShapeDtypeStruct(shape, F32) for shape in shapes),
        in_specs=[near, near],
        out_specs=(far, far),
        scratch_shapes=[dma((2,))],
        compiler_params=pltpu.CompilerParams(vmem_limit_bytes=59 << 20),
    )(pltpu.with_memory_space_constraint(core_t, pltpu.VMEM), pltpu.with_memory_space_constraint(gram, pltpu.VMEM))
    return core_t.T, gram


def solution(mesh):
    in_specs = (P("gx", "gy", "ta"), P("ta", None), P("gy", None), P("gx", None))
    out_specs = (P(None, ("gx", "gy", "ta")), P(("gx", "gy", "ta"), None))
    return jax.shard_map(shards, mesh=mesh, in_specs=in_specs, out_specs=out_specs, check_vma=False)
```

```python
import functools

import jax
import jax.numpy as jnp
from jax import lax
from jax.experimental import pallas as pl
from jax.experimental.pallas import tpu as pltpu
from jax.sharding import PartitionSpec as P

F32 = jnp.float32
BF16 = jnp.bfloat16
MESH = pl.DeviceIdType.MESH
NN = (((1,), (0,)), ((), ()))
NT = (((1,), (1,)), ((), ()))
SIZES = (2, 2, 2, 2)
CHUNKS = tuple((sum(SIZES[:c]), SIZES[c]) for c in range(len(SIZES)))
EARLY = 2
ROUNDS = ((0, 1), (1, 1))


def split(values):
    high = values.astype(BF16)
    return high, (values - high.astype(F32)).astype(BF16)


def dot(a, b, dims):
    return lax.dot_general(a, b, dims, preferred_element_type=F32)


def exchange(values, lane, unit, stages):
    for s in stages:
        low = (lane // (unit * s)) % 2 == 0
        out = list(values)
        for a in range(len(values)):
            if a & s:
                continue
            out[a] = jnp.where(low, values[a], pltpu.roll(values[a + s], unit * s, 1))
            out[a + s] = jnp.where(low, pltpu.roll(values[a], 128 - unit * s, 1), values[a + s])
        values = out
    return values


def kernel(
    elev, time_t, north_t, east_t, core_out, gram_out,
    slab, time_v, north_v, basis, send1, recv1, gathered, mate_tiles, halves, columns, easts, core_part, core_mates, send2, recv2,
    slab_sem, small_sem, send1_sem, recv1_sem, gather_send, gather_recv, mate_send, mate_recv,
    east_send, east_recv, core_send, core_recv, send2_sem, recv2_sem,
):
    gx, gy, ta = lax.axis_index("gx"), lax.axis_index("gy"), lax.axis_index("ta")
    z, core = gx // 2, gx % 2
    y, x = gy // 2, ta * 2 + gy % 2
    near, beyond = z + 1 - 2 * (z % 2), (z + 3 + 2 * (z % 2)) % 4
    mates = [z2 * 2 + c2 for z2 in (z, near) for c2 in (core, 1 - core)]
    gathered_by = [(z2 * 2 + c2, z3 * 2 + c2) for z2, z3 in ((z, beyond), (near, (z + 2) % 4)) for c2 in (core, 1 - core)]

    def slab_copy(c):
        part = pl.ds(*CHUNKS[c])
        return pltpu.make_async_copy(elev.at[:, part], slab.at[:, part], slab_sem.at[c])

    small = [
        pltpu.make_async_copy(time_t, time_v, small_sem.at[0]),
        pltpu.make_async_copy(north_t, north_v, small_sem.at[1]),
        pltpu.make_async_copy(east_t, easts.at[0], small_sem.at[2]),
    ]
    for copy in small:
        copy.start()
    for c in range(2):
        slab_copy(c).start()

    plane, sheet = [], []
    for slot in range(1, 16):
        y2, x2 = (y + slot // 4) % 4, (x + slot % 4) % 4
        plane.append((slot, (gx, y2 * 2 + x2 % 2, x2 // 2), y2, x2))
    for zs in (1, 0):
        for ys in (2, 1, 3, 0):
            if zs or ys:
                y2 = (y + ys) % 4
                sheet.append((zs, (gathered_by[0][zs], y2 * 2 + gy % 2, ta)))
    rings = []
    for m in range(4):
        ring = []
        for slot in (2, 1, 3, 0):
            x2 = (x + slot) % 4
            ring.append((slot, (mates[m], y * 2 + x2 % 2, x2 // 2), x2))
        rings.append(ring if m else ring[:3])
    across = rings[1] + rings[2] + rings[3]
    far_first = sorted(plane, key=lambda p: -((0, 1, 2, 1)[p[0] // 4] + (0, 1, 2, 1)[p[0] % 4]))
    barrier = pltpu.get_barrier_semaphore()
    peers = [p[1] for p in plane + across] + [device for zs, device in sheet if zs]
    for device in peers:
        pl.semaphore_signal(barrier, inc=1, device_id=device, device_id_type=MESH)

    for copy in small:
        copy.wait()
    time_high, time_low = split(time_v[...])
    time_both = jnp.concatenate([time_high, time_low], 0)
    time_wide = time_high.astype(F32).T.astype(BF16)
    lane64 = lax.broadcasted_iota(jnp.int32, (64, 128), 1)

    def make_basis():
        row = lax.broadcasted_iota(jnp.int32, (32, 128), 0)
        lane = lax.broadcasted_iota(jnp.int32, (32, 128), 1)
        spread = jnp.where(lane // 4 == row, 1.0, 0.0).astype(BF16)
        for h, part in enumerate(split(north_v[...].T)):
            wide = dot(part, spread, NN)
            for x4 in range(4):
                own = jnp.where(lane64 % 4 == x4, wide, 0.0).astype(BF16)
                basis[pl.ds(x4 * 64, 64), pl.ds(h * 128, 128)] = own

    def over_time(g, b):
        high, low = split(slab[b, g])
        t = dot(time_both, high, NT)
        return t[:32] + t[32:] + dot(low, time_wide, NN).T

    def over_y(terms):
        high, low = zip(*[split(t) for t in terms])
        r = dot(jnp.concatenate(high, 0), basis[...], NN)
        return r[:, :128] + r[:, 128:] + dot(jnp.concatenate(low, 0), basis[:, :128], NN)

    def remote(src, dst, send_sem, recv_sem, device):
        return pltpu.make_async_remote_copy(
            src_ref=src, dst_ref=dst, send_sem=send_sem, recv_sem=recv_sem, device_id=device, device_id_type=MESH
        )

    def await_bytes(ref, sem):
        pltpu.make_async_copy(ref, ref, sem).wait()

    def place(qg):
        return (qg % 2) * 2 + qg // 2

    def finish(c, terms):
        start, count = CHUNKS[c]
        for k in range(count):
            sums = over_y(terms[k])
            for b in range(4):
                for qg in range(4):
                    at = b * 32 + qg * 8
                    send1[b, place(qg), start + k] = sums[at : at + 8]
        if c == 0:
            pl.semaphore_wait(barrier, 31)
        part = pl.ds(start, count)
        for slot, device, y2, x2 in far_first:
            remote(
                send1.at[y2, x2, part], recv1.at[slot, part], send1_sem.at[c], recv1_sem.at[c], device
            ).start()
        if c == 0:
            for zs, device in sheet[3:4]:
                remote(easts.at[0], easts.at[1], east_send, east_recv, device).start()

    make_basis()
    for c, (start, count) in enumerate(CHUNKS):
        slab_copy(c).wait()
        if c + 2 < len(CHUNKS):
            slab_copy(c + 2).start()
        finish(c, [[over_time(start + k, b) for b in range(4)] for k in range(count)])

    lane8 = lax.broadcasted_iota(jnp.int32, (8, 128), 1)
    own = []
    for c, (start, count) in enumerate(CHUNKS):
        part = pl.ds(start, count)
        await_bytes(recv1.at[pl.ds(1, 15), part], recv1_sem.at[c])
        totals = []
        for g in range(start, start + count):
            total = send1[y, x, g]
            for slot in range(1, 16):
                total = total + recv1[slot, g]
            totals.append(total)
        totals = exchange(totals, lane8, 4, (1,))
        own += totals
        for k in range(count):
            gathered[0, y, start + k] = totals[k]
        for zs, device in sheet:
            remote(
                gathered.at[0, y, part], gathered.at[zs, y, part], gather_send, gather_recv.at[zs, c // EARLY], device
            ).start()
        for m in range(1, 4):
            remote(gathered.at[0, y, part], mate_tiles.at[m - 1, part], mate_send, mate_recv, rings[m][3][1]).start()

    def left_side(tiles):
        turned = jnp.concatenate(exchange(tiles, lane8, 4, (4, 2)), 0).T
        high, low = split(jnp.concatenate([turned[32 * k : 32 * k + 32] for k in range(4)], 1))
        return jnp.concatenate([high, high, low], 1)

    def half(zs, h):
        by_y = [exchange([gathered[zs, y2, h * 4 + g] for g in range(4)], lane8, 4, (2,)) for y2 in range(4)]
        by_low = [exchange([by_y[y2][k] for y2 in range(4)], lane8, 32, (2, 1)) for k in range(4)]
        return [[by_low[k][high_p] for k in range(4)] for high_p in range(4)]

    def await_half(zs, h):
        ref = gathered.at[0, pl.ds(0, 3), pl.ds(0, 4)] if zs == 0 else gathered.at[zs, :, pl.ds(0, 4)]
        await_bytes(ref, gather_recv.at[zs, h])

    lefts = [left_side(own)]
    for zs in range(2):
        await_half(zs, 0)
    for zs in range(2):
        tiles = half(zs, 0)
        for high_p in range(4):
            for k in range(4):
                halves[zs, high_p, k] = tiles[high_p][k]
    await_bytes(mate_tiles, mate_recv)
    for m in range(3):
        lefts.append(left_side([mate_tiles[m, g] for g in range(8)]))
    left = jnp.concatenate(lefts, 0)

    for r, (start, count) in enumerate(ROUNDS):
        for zs in range(start, start + count):
            await_half(zs, 1)
        for zs in range(start, start + count):
            second = half(zs, 1)
            tiles = [None] * 32
            for high_p in range(4):
                for k in range(4):
                    pair = exchange([halves[zs, high_p, k], second[high_p][k]], lane8, 16, (1,))
                    tiles[high_p * 8 + k], tiles[high_p * 8 + 4 + k] = pair
            for p in range(32):
                columns[zs, p] = tiles[p]
            high, low = split(jnp.concatenate(tiles, 0))
            product = dot(left, jnp.concatenate([high, low, high], 0), NN)
            for m in range(4):
                for qg in range(4):
                    at = m * 32 + qg * 8
                    send2[m, place(qg), zs] = product[at : at + 8]
        part = pl.ds(start, count)
        for m in (3, 2, 1, 0):
            for slot, device, at in rings[m]:
                remote(
                    send2.at[m, at, part], recv2.at[m, slot, part], send2_sem.at[r, m], recv2_sem.at[r, m], device
                ).start()

    await_bytes(easts.at[1], east_recv)
    rows = [jnp.concatenate([columns[zs, 4 * mates[m] + y] for m in range(4)], 0) for zs in range(2)]
    core_sum = lax.dot_general(
        jnp.concatenate(rows, 1),
        jnp.concatenate([easts[zs] for zs in range(2)], 1),
        NT,
        precision=lax.Precision.HIGHEST,
        preferred_element_type=F32,
    )
    core_part[...] = jnp.zeros((3, 8, 128), F32)
    core_copies = []
    for m in range(1, 4):
        core_part[m - 1, :, :32] = core_sum[8 * m : 8 * m + 8]
        core_copies.append(
            remote(core_part.at[m - 1], core_mates.at[m - 1], core_send.at[m - 1], core_recv.at[m - 1], rings[m][3][1])
        )
    for copy in core_copies:
        copy.start()
    total = core_sum[:8]
    for m in range(3):
        core_copies[m].wait_recv()
        total = total + core_mates[m, :, :32]
    core_out[...] = total

    inverse_count = 1.0 / 1024.0

    for r, (start, count) in enumerate(ROUNDS):
        part = pl.ds(start, count)
        for m in range(4):
            peers = range(4) if m else range(1, 4)
            await_bytes(recv2.at[m, pl.ds(peers[0], len(peers)), part], recv2_sem.at[r, m])
            for zs in range(start, start + count):
                total = recv2[m, 0, zs] if m else send2[0, x, zs]
                for slot in range(1, 4):
                    total = total + recv2[m, slot, zs]
                at = gathered_by[m][zs] * 128
                gram_out[:, pl.ds(pl.multiple_of(at, 128), 128)] = total * inverse_count

    for c, part in enumerate(CHUNKS):
        await_bytes(recv1.at[pl.ds(1, 15), pl.ds(*part)], send1_sem.at[c])
    await_bytes(recv1.at[pl.ds(1, 7)], gather_send)
    await_bytes(mate_tiles, mate_send)
    await_bytes(easts.at[1], east_send)
    for copy in core_copies:
        copy.wait_send()
    for r, part in enumerate(ROUNDS):
        for m in range(4):
            peers = range(4) if m else range(1, 4)
            await_bytes(recv2.at[m, pl.ds(peers[0], len(peers)), pl.ds(*part)], send2_sem.at[r, m])


def hand_over(core_in, gram_in, core_out, gram_out, sem):
    copies = [
        pltpu.make_async_copy(core_in, core_out, sem.at[0]),
        pltpu.make_async_copy(gram_in, gram_out, sem.at[1]),
    ]
    for copy in copies:
        copy.start()
    for copy in copies:
        copy.wait()


def shards(elevations, time_basis, north_basis, east_basis):
    dma = pltpu.SemaphoreType.DMA
    shapes = ((8, 32), (8, 1024))
    far = pl.BlockSpec(memory_space=pltpu.HBM)
    near = pl.BlockSpec(memory_space=pltpu.VMEM)
    chunks = len(CHUNKS)
    core_t, gram = pl.pallas_call(
        kernel,
        out_shape=tuple(pltpu.VMEM(shape, F32) for shape in shapes),
        in_specs=[far] * 4,
        out_specs=(near, near),
        scratch_shapes=[
            pltpu.VMEM((4, 8, 256, 512), F32),
            pltpu.VMEM((32, 512), F32),
            pltpu.VMEM((32, 64), F32),
            pltpu.VMEM((256, 256), BF16),
            pltpu.VMEM((4, 4, 8, 8, 128), F32),
            pltpu.VMEM((16, 8, 8, 128), F32),
            pltpu.VMEM((2, 4, 8, 8, 128), F32),
            pltpu.VMEM((3, 8, 8, 128), F32),
            pltpu.VMEM((2, 4, 4, 8, 128), F32),
            pltpu.VMEM((2, 32, 8, 128), F32),
            pltpu.VMEM((2, 32, 128), F32),
            pltpu.VMEM((3, 8, 128), F32),
            pltpu.VMEM((3, 8, 128), F32),
            pltpu.VMEM((4, 4, 2, 8, 128), F32),
            pltpu.VMEM((4, 4, 2, 8, 128), F32),
            dma((chunks,)),
            dma((3,)),
            dma((chunks,)),
            dma((chunks,)),
            dma,
            dma((2, 2)),
            dma,
            dma,
            dma,
            dma,
            dma((3,)),
            dma((3,)),
            dma((2, 4)),
            dma((2, 4)),
        ],
        compiler_params=pltpu.CompilerParams(
            collective_id=0, has_side_effects=True, vmem_limit_bytes=59 << 20
        ),
    )(elevations.reshape(4, 8, 256, 512), time_basis.T, north_basis.T, east_basis.T)
    core_t, gram = pl.pallas_call(
        hand_over,
        out_shape=tuple(jax.ShapeDtypeStruct(shape, F32) for shape in shapes),
        in_specs=[near, near],
        out_specs=(far, far),
        scratch_shapes=[dma((2,))],
        compiler_params=pltpu.CompilerParams(vmem_limit_bytes=59 << 20),
    )(pltpu.with_memory_space_constraint(core_t, pltpu.VMEM), pltpu.with_memory_space_constraint(gram, pltpu.VMEM))
    return core_t.T, gram


def solution(mesh):
    in_specs = (P("gx", "gy", "ta"), P("ta", None), P("gy", None), P("gx", None))
    out_specs = (P(None, ("gx", "gy", "ta")), P(("gx", "gy", "ta"), None))
    return jax.shard_map(shards, mesh=mesh, in_specs=in_specs, out_specs=out_specs, check_vma=False)
```

```python
import functools

import jax
import jax.numpy as jnp
from jax import lax
from jax.experimental import pallas as pl
from jax.experimental.pallas import tpu as pltpu
from jax.sharding import PartitionSpec as P

F32 = jnp.float32
BF16 = jnp.bfloat16
MESH = pl.DeviceIdType.MESH
NN = (((1,), (0,)), ((), ()))
NT = (((1,), (1,)), ((), ()))
SIZES = (2, 2, 2, 2)
CHUNKS = tuple((sum(SIZES[:c]), SIZES[c]) for c in range(len(SIZES)))
LAST = len(CHUNKS) - 1
EARLY = 2
ROUNDS = ((0, 1), (1, 1))


def split(values):
    high = values.astype(BF16)
    return high, (values - high.astype(F32)).astype(BF16)


def dot(a, b, dims):
    return lax.dot_general(a, b, dims, preferred_element_type=F32)


def exchange(values, lane, unit, stages):
    for s in stages:
        low = (lane // (unit * s)) % 2 == 0
        out = list(values)
        for a in range(len(values)):
            if a & s:
                continue
            out[a] = jnp.where(low, values[a], pltpu.roll(values[a + s], unit * s, 1))
            out[a + s] = jnp.where(low, pltpu.roll(values[a], 128 - unit * s, 1), values[a + s])
        values = out
    return values


def kernel(
    elev, time_t, north_t, east_t, core_out, gram_out,
    slab, time_v, north_v, basis, send1, recv1, gathered, mate_tiles, halves, columns, easts, core_part, core_mates, send2, recv2,
    slab_sem, small_sem, send1_sem, recv1_sem, gather_send, gather_recv, mate_send, mate_recv,
    east_send, east_recv, core_send, core_recv, send2_sem, recv2_sem,
):
    gx, gy, ta = lax.axis_index("gx"), lax.axis_index("gy"), lax.axis_index("ta")
    z, core = gx // 2, gx % 2
    y, x = gy // 2, ta * 2 + gy % 2
    near, beyond = z + 1 - 2 * (z % 2), (z + 3 + 2 * (z % 2)) % 4
    mates = [z2 * 2 + c2 for z2 in (z, near) for c2 in (core, 1 - core)]
    gathered_by = [(z2 * 2 + c2, z3 * 2 + c2) for z2, z3 in ((z, beyond), (near, (z + 2) % 4)) for c2 in (core, 1 - core)]

    def slab_copy(c):
        if c < LAST:
            part = pl.ds(*CHUNKS[c])
            return pltpu.make_async_copy(elev.at[:, part], slab.at[:, part], slab_sem.at[c])
        part, times = pl.ds(*CHUNKS[LAST]), pl.ds((c - LAST) * 256, 256)
        return pltpu.make_async_copy(elev.at[:, part, :, times], slab.at[:, part, :, times], slab_sem.at[c])

    small = [
        pltpu.make_async_copy(time_t, time_v, small_sem.at[0]),
        pltpu.make_async_copy(north_t, north_v, small_sem.at[1]),
        pltpu.make_async_copy(east_t, easts.at[0], small_sem.at[2]),
    ]
    for copy in small:
        copy.start()
    for c in range(2):
        slab_copy(c).start()

    plane, sheet = [], []
    for slot in range(1, 16):
        y2, x2 = (y + slot // 4) % 4, (x + slot % 4) % 4
        plane.append((slot, (gx, y2 * 2 + x2 % 2, x2 // 2), y2, x2))
    for zs in (1, 0):
        for ys in (2, 1, 3, 0):
            if zs or ys:
                y2 = (y + ys) % 4
                sheet.append((zs, (gathered_by[0][zs], y2 * 2 + gy % 2, ta)))
    rings = []
    for m in range(4):
        ring = []
        for slot in (2, 1, 3, 0):
            x2 = (x + slot) % 4
            ring.append((slot, (mates[m], y * 2 + x2 % 2, x2 // 2), x2))
        rings.append(ring if m else ring[:3])
    across = rings[1] + rings[2] + rings[3]
    far_first = sorted(plane, key=lambda p: -((0, 1, 2, 1)[p[0] // 4] + (0, 1, 2, 1)[p[0] % 4]))
    barrier = pltpu.get_barrier_semaphore()
    peers = [p[1] for p in plane + across] + [device for zs, device in sheet if zs]
    for device in peers:
        pl.semaphore_signal(barrier, inc=1, device_id=device, device_id_type=MESH)

    for copy in small:
        copy.wait()
    time_high, time_low = split(time_v[...])
    time_both = jnp.concatenate([time_high, time_low], 0)
    time_wide = time_high.astype(F32).T.astype(BF16)
    lane64 = lax.broadcasted_iota(jnp.int32, (64, 128), 1)

    def make_basis():
        row = lax.broadcasted_iota(jnp.int32, (32, 128), 0)
        lane = lax.broadcasted_iota(jnp.int32, (32, 128), 1)
        spread = jnp.where(lane // 4 == row, 1.0, 0.0).astype(BF16)
        for h, part in enumerate(split(north_v[...].T)):
            wide = dot(part, spread, NN)
            for x4 in range(4):
                own = jnp.where(lane64 % 4 == x4, wide, 0.0).astype(BF16)
                basis[pl.ds(x4 * 64, 64), pl.ds(h * 128, 128)] = own

    def over_time(g, b, first=0, last=512):
        high, low = split(slab[b, g, :, first:last])
        t = dot(time_both[:, first:last], high, NT)
        return t[:32] + t[32:] + dot(low, time_wide[first:last], NN).T

    def over_y(terms):
        high, low = zip(*[split(t) for t in terms])
        r = dot(jnp.concatenate(high, 0), basis[...], NN)
        return r[:, :128] + r[:, 128:] + dot(jnp.concatenate(low, 0), basis[:, :128], NN)

    def remote(src, dst, send_sem, recv_sem, device):
        return pltpu.make_async_remote_copy(
            src_ref=src, dst_ref=dst, send_sem=send_sem, recv_sem=recv_sem, device_id=device, device_id_type=MESH
        )

    def await_bytes(ref, sem):
        pltpu.make_async_copy(ref, ref, sem).wait()

    def place(qg):
        return (qg % 2) * 2 + qg // 2

    def finish(c, terms):
        start, count = CHUNKS[c]
        for k in range(count):
            sums = over_y(terms[k])
            for b in range(4):
                for qg in range(4):
                    at = b * 32 + qg * 8
                    send1[b, place(qg), start + k] = sums[at : at + 8]
        if c == 0:
            pl.semaphore_wait(barrier, 31)
        part = pl.ds(start, count)
        for slot, device, y2, x2 in far_first:
            remote(
                send1.at[y2, x2, part], recv1.at[slot, part], send1_sem.at[c], recv1_sem.at[c], device
            ).start()
        if c == 0:
            for zs, device in sheet[3:4]:
                remote(easts.at[0], easts.at[1], east_send, east_recv, device).start()

    make_basis()
    for c, (start, count) in enumerate(CHUNKS):
        slab_copy(c).wait()
        if c + 2 <= LAST + 1:
            slab_copy(c + 2).start()
        if c < LAST:
            finish(c, [[over_time(start + k, b) for b in range(4)] for k in range(count)])
    start, count = CHUNKS[LAST]
    early = [[over_time(start + k, b, 0, 256) for b in range(4)] for k in range(count)]
    slab_copy(LAST + 1).wait()
    finish(LAST, [[early[k][b] + over_time(start + k, b, 256, 512) for b in range(4)] for k in range(count)])

    lane8 = lax.broadcasted_iota(jnp.int32, (8, 128), 1)
    own = []
    for c, (start, count) in enumerate(CHUNKS):
        part = pl.ds(start, count)
        await_bytes(recv1.at[pl.ds(1, 15), part], recv1_sem.at[c])
        totals = []
        for g in range(start, start + count):
            total = send1[y, x, g]
            for slot in range(1, 16):
                total = total + recv1[slot, g]
            totals.append(total)
        totals = exchange(totals, lane8, 4, (1,))
        own += totals
        for k in range(count):
            gathered[0, y, start + k] = totals[k]
        for zs, device in sheet:
            remote(
                gathered.at[0, y, part], gathered.at[zs, y, part], gather_send, gather_recv.at[zs, c // EARLY], device
            ).start()
        for m in range(1, 4):
            remote(gathered.at[0, y, part], mate_tiles.at[m - 1, part], mate_send, mate_recv, rings[m][3][1]).start()

    def left_side(tiles):
        turned = jnp.concatenate(exchange(tiles, lane8, 4, (4, 2)), 0).T
        high, low = split(jnp.concatenate([turned[32 * k : 32 * k + 32] for k in range(4)], 1))
        return jnp.concatenate([high, high, low], 1)

    def half(zs, h):
        by_y = [exchange([gathered[zs, y2, h * 4 + g] for g in range(4)], lane8, 4, (2,)) for y2 in range(4)]
        by_low = [exchange([by_y[y2][k] for y2 in range(4)], lane8, 32, (2, 1)) for k in range(4)]
        return [[by_low[k][high_p] for k in range(4)] for high_p in range(4)]

    def await_half(zs, h):
        ref = gathered.at[0, pl.ds(0, 3), pl.ds(0, 4)] if zs == 0 else gathered.at[zs, :, pl.ds(0, 4)]
        await_bytes(ref, gather_recv.at[zs, h])

    lefts = [left_side(own)]
    for zs in range(2):
        await_half(zs, 0)
    for zs in range(2):
        tiles = half(zs, 0)
        for high_p in range(4):
            for k in range(4):
                halves[zs, high_p, k] = tiles[high_p][k]
    await_bytes(mate_tiles, mate_recv)
    for m in range(3):
        lefts.append(left_side([mate_tiles[m, g] for g in range(8)]))
    left = jnp.concatenate(lefts, 0)

    for r, (start, count) in enumerate(ROUNDS):
        for zs in range(start, start + count):
            await_half(zs, 1)
        for zs in range(start, start + count):
            second = half(zs, 1)
            tiles = [None] * 32
            for high_p in range(4):
                for k in range(4):
                    pair = exchange([halves[zs, high_p, k], second[high_p][k]], lane8, 16, (1,))
                    tiles[high_p * 8 + k], tiles[high_p * 8 + 4 + k] = pair
            for p in range(32):
                columns[zs, p] = tiles[p]
            high, low = split(jnp.concatenate(tiles, 0))
            product = dot(left, jnp.concatenate([high, low, high], 0), NN)
            for m in range(4):
                for qg in range(4):
                    at = m * 32 + qg * 8
                    send2[m, place(qg), zs] = product[at : at + 8]
        part = pl.ds(start, count)
        for m in (3, 2, 1, 0):
            for slot, device, at in rings[m]:
                remote(
                    send2.at[m, at, part], recv2.at[m, slot, part], send2_sem.at[r, m], recv2_sem.at[r, m], device
                ).start()

    await_bytes(easts.at[1], east_recv)
    rows = [jnp.concatenate([columns[zs, 4 * mates[m] + y] for m in range(4)], 0) for zs in range(2)]
    core_sum = lax.dot_general(
        jnp.concatenate(rows, 1),
        jnp.concatenate([easts[zs] for zs in range(2)], 1),
        NT,
        precision=lax.Precision.HIGHEST,
        preferred_element_type=F32,
    )
    core_part[...] = jnp.zeros((3, 8, 128), F32)
    core_copies = []
    for m in range(1, 4):
        core_part[m - 1, :, :32] = core_sum[8 * m : 8 * m + 8]
        core_copies.append(
            remote(core_part.at[m - 1], core_mates.at[m - 1], core_send.at[m - 1], core_recv.at[m - 1], rings[m][3][1])
        )
    for copy in core_copies:
        copy.start()
    total = core_sum[:8]
    for m in range(3):
        core_copies[m].wait_recv()
        total = total + core_mates[m, :, :32]
    core_out[...] = total

    inverse_count = 1.0 / 1024.0

    for r, (start, count) in enumerate(ROUNDS):
        part = pl.ds(start, count)
        for m in range(4):
            peers = range(4) if m else range(1, 4)
            await_bytes(recv2.at[m, pl.ds(peers[0], len(peers)), part], recv2_sem.at[r, m])
            for zs in range(start, start + count):
                total = recv2[m, 0, zs] if m else send2[0, x, zs]
                for slot in range(1, 4):
                    total = total + recv2[m, slot, zs]
                at = gathered_by[m][zs] * 128
                gram_out[:, pl.ds(pl.multiple_of(at, 128), 128)] = total * inverse_count

    for c, part in enumerate(CHUNKS):
        await_bytes(recv1.at[pl.ds(1, 15), pl.ds(*part)], send1_sem.at[c])
    await_bytes(recv1.at[pl.ds(1, 7)], gather_send)
    await_bytes(mate_tiles, mate_send)
    await_bytes(easts.at[1], east_send)
    for copy in core_copies:
        copy.wait_send()
    for r, part in enumerate(ROUNDS):
        for m in range(4):
            peers = range(4) if m else range(1, 4)
            await_bytes(recv2.at[m, pl.ds(peers[0], len(peers)), pl.ds(*part)], send2_sem.at[r, m])


def hand_over(core_in, gram_in, core_out, gram_out, sem):
    copies = [
        pltpu.make_async_copy(core_in, core_out, sem.at[0]),
        pltpu.make_async_copy(gram_in, gram_out, sem.at[1]),
    ]
    for copy in copies:
        copy.start()
    for copy in copies:
        copy.wait()


def shards(elevations, time_basis, north_basis, east_basis):
    dma = pltpu.SemaphoreType.DMA
    shapes = ((8, 32), (8, 1024))
    far = pl.BlockSpec(memory_space=pltpu.HBM)
    near = pl.BlockSpec(memory_space=pltpu.VMEM)
    chunks = len(CHUNKS)
    core_t, gram = pl.pallas_call(
        kernel,
        out_shape=tuple(pltpu.VMEM(shape, F32) for shape in shapes),
        in_specs=[far] * 4,
        out_specs=(near, near),
        scratch_shapes=[
            pltpu.VMEM((4, 8, 256, 512), F32),
            pltpu.VMEM((32, 512), F32),
            pltpu.VMEM((32, 64), F32),
            pltpu.VMEM((256, 256), BF16),
            pltpu.VMEM((4, 4, 8, 8, 128), F32),
            pltpu.VMEM((16, 8, 8, 128), F32),
            pltpu.VMEM((2, 4, 8, 8, 128), F32),
            pltpu.VMEM((3, 8, 8, 128), F32),
            pltpu.VMEM((2, 4, 4, 8, 128), F32),
            pltpu.VMEM((2, 32, 8, 128), F32),
            pltpu.VMEM((2, 32, 128), F32),
            pltpu.VMEM((3, 8, 128), F32),
            pltpu.VMEM((3, 8, 128), F32),
            pltpu.VMEM((4, 4, 2, 8, 128), F32),
            pltpu.VMEM((4, 4, 2, 8, 128), F32),
            dma((chunks + 1,)),
            dma((3,)),
            dma((chunks,)),
            dma((chunks,)),
            dma,
            dma((2, 2)),
            dma,
            dma,
            dma,
            dma,
            dma((3,)),
            dma((3,)),
            dma((2, 4)),
            dma((2, 4)),
        ],
        compiler_params=pltpu.CompilerParams(
            collective_id=0, has_side_effects=True, vmem_limit_bytes=59 << 20
        ),
    )(elevations.reshape(4, 8, 256, 512), time_basis.T, north_basis.T, east_basis.T)
    core_t, gram = pl.pallas_call(
        hand_over,
        out_shape=tuple(jax.ShapeDtypeStruct(shape, F32) for shape in shapes),
        in_specs=[near, near],
        out_specs=(far, far),
        scratch_shapes=[dma((2,))],
        compiler_params=pltpu.CompilerParams(vmem_limit_bytes=59 << 20),
    )(pltpu.with_memory_space_constraint(core_t, pltpu.VMEM), pltpu.with_memory_space_constraint(gram, pltpu.VMEM))
    return core_t.T, gram


def solution(mesh):
    in_specs = (P("gx", "gy", "ta"), P("ta", None), P("gy", None), P("gx", None))
    out_specs = (P(None, ("gx", "gy", "ta")), P(("gx", "gy", "ta"), None))
    return jax.shard_map(shards, mesh=mesh, in_specs=in_specs, out_specs=out_specs, check_vma=False)
```
